32 devices in a mesh: row: 2 (over y), col: 16 (over z, x, core).
Axes of the slice: x: 2, y: 2, z: 4, core: 2. Of those that a mesh axis runs over, the one named last changes fastest.
Arguments:
- strip: float32 [12, 2048, 2, 1024], P(None, 'col', None, 'row'), may hold values from -6 to 6
- lower: float32 [12, 2048, 2, 1024], P(None, 'col', None, 'row'), may hold values from -1.6 to 1.6, as said below
Outputs:
- reduced: float32 [12, 2048, 2, 1024], P(None, 'col', None, 'row')
The draws below stay inside these ranges and needn't reach their ends.
Inputs may be any that keep to these rules, and one draw needn't show every extreme that they name: `lower`: in the first 2048 rows the diagonal lies between 0.8 and 1.6 and entries above it are zero.
All inputs are finite; a program needn't handle non-finite values.
Results may differ from the reference program's by a relative error of at most 0.00013.
Values sent between devices are 32-bit elements; how exact they have to be, the bound alone decides.
A program may use at most 128 MiB of HBM per device.

```python
import math
import jax
import jax.numpy as jnp
from jax import lax

NB = 1024
ROUNDS = 12


def draw_lower(key, part):
    key_main, key_diag = jax.random.split(key)
    shape = (ROUNDS, 2 * NB, 2, NB)
    noise = jnp.clip(jax.random.normal(key_main, shape, jnp.float32), -6.0, 6.0)
    diag_values = jax.random.uniform(key_diag, shape, jnp.float32, 0.8, 1.6)
    row_index = lax.broadcasted_iota(jnp.int32, shape, 0) * (2 * NB) + lax.broadcasted_iota(jnp.int32, shape, 1)
    col_block = lax.broadcasted_iota(jnp.int32, shape, 2)
    col_inner = lax.broadcasted_iota(jnp.int32, shape, 3)
    row_block = row_index // NB
    row_inner = row_index % NB
    in_lead = row_index < 2 * NB
    strict_lower = jnp.where(col_inner < row_inner, 0.6 / math.sqrt(NB) * noise, 0.0)
    diag_part = jnp.where(col_inner == row_inner, diag_values, strict_lower)
    cross_value = 0.8 / math.sqrt(NB) * noise
    lead_value = jnp.where(row_block == col_block, diag_part, jnp.where(row_block > col_block, cross_value, 0.0))
    trail_value = noise / math.sqrt(2 * NB)
    return jnp.where(in_lead, lead_value, trail_value)


def block_levels(stream_key, dims, pieces, smallest, largest):
    factor_of = 1.0
    for dim, blocks in pieces:
        heights = jax.random.uniform(jax.random.fold_in(jax.random.fold_in(stream_key, 6), dim), (blocks,), jnp.float32, smallest / len(pieces), largest / len(pieces))
        factor_of = factor_of * jnp.repeat(jnp.exp(heights), dims[dim] // blocks).reshape((-1,) + (1,) * (len(dims) - 1 - dim))
    return factor_of


def bell_draw(rng, shape, spread, reach, cuts=(), dtype=jnp.bfloat16):
    factor_of = block_levels(rng, shape, cuts, -0.22, 0.18) if cuts else 1.0
    values = jax.random.normal(rng, shape, jnp.float32) * spread * factor_of
    return jnp.minimum(jnp.maximum(values, -reach), reach).astype(dtype)


def setup_inputs(seed: int = 0) -> dict:
    keys = jax.random.split(jax.random.key(seed), 3)
    return {
        "strip": bell_draw(keys[0], (ROUNDS, 2 * NB, 2, NB), 1.0, 6.0, ((1, 16), (3, 2)), jnp.float32),
        "lower": draw_lower(jax.random.fold_in(keys[2], 71), 0),
    }


highest = lax.Precision.HIGHEST


def multiply_full(left_side, right_side):
    return jnp.dot(left_side, right_side, precision=highest, preferred_element_type=jnp.float32)


def reference(strip, lower):
    full_strip = strip.reshape(ROUNDS * 2 * NB, 2 * NB)
    factors = lower.reshape(ROUNDS * 2 * NB, 2 * NB)
    first_inverse = factors[:NB, :NB]
    cross_part = factors[NB:2 * NB, :NB]
    second_inverse = factors[NB:2 * NB, NB:2 * NB]
    below_part = factors[2 * NB:, :]
    upper_half = multiply_full(first_inverse, full_strip[:, :NB].T)
    remainder = full_strip[:, NB:].T - multiply_full(cross_part, upper_half)
    lower_half = multiply_full(second_inverse, remainder)
    solved = jnp.concatenate([upper_half.T, lower_half.T], axis=1)
    lead_rows = solved[:2 * NB]
    lead_first = multiply_full(first_inverse, lead_rows[:NB])
    lead_second = multiply_full(second_inverse, lead_rows[NB:] - multiply_full(cross_part, lead_first))
    lead_block = jnp.concatenate([lead_first, lead_second], axis=0)
    trail_rows = solved[2 * NB:] - multiply_full(below_part, lead_block)
    return jnp.concatenate([lead_block, trail_rows], axis=0).reshape(ROUNDS, 2 * NB, 2, NB)
```

```python
import jax
import jax.numpy as jnp
from jax import lax
from jax.sharding import PartitionSpec as P

PREC = lax.Precision.HIGH


def mm(a, b):
    return jnp.dot(a, b, precision=PREC, preferred_element_type=jnp.float32)


def mm_t(a, b):
    return lax.dot_general(
        a, b, (((1,), (1,)), ((), ())), precision=PREC, preferred_element_type=jnp.float32
    )


def row_parts(x):
    n = lax.axis_size("row")
    parts = [x]
    for s in range(1, n):
        parts.append(lax.ppermute(x, "row", [((i + s) % n, i) for i in range(n)]))
    return parts


def in_order(parts, r):
    n = len(parts)
    twice = jnp.stack(parts + parts[:-1], axis=0)
    return lax.dynamic_slice_in_dim(twice, (n - r) % n, n, 0)


def local(strip, lower):
    rounds, width, _, run = strip.shape
    n_row = lax.axis_size("row")
    n_col = lax.axis_size("col")
    block = run * n_row
    r = lax.axis_index("row")
    c = lax.axis_index("col")
    half = n_col // 2
    tail = (rounds - 1) * width

    lead_l = lower[0]
    first = lax.all_gather(lead_l[:, 0, :], ("col", "row"), axis=0)
    first = first.reshape(n_col, n_row, width, run).transpose(0, 2, 1, 3).reshape(2 * block, block)
    e0, f = first[:block], first[block:]
    e1_mine = lead_l[:, 1, :]
    cut = width // 2
    moved = lax.ppermute(e1_mine[:cut], "col", [(half + i, i) for i in range(half)])
    e1_share = jnp.where(c < half, moved, e1_mine[cut:])
    second = lax.all_gather(e1_share, ("col", "row"), axis=0)
    second = second.reshape(2, half, n_row, cut, run).transpose(1, 0, 3, 2, 4)
    e1 = second.reshape(block, block)

    lead_s = in_order(row_parts(strip[0]), r)
    s0 = lead_s[:, :, 0, :].transpose(1, 0, 2).reshape(width, block)
    s1 = lead_s[:, :, 1, :].transpose(1, 0, 2).reshape(width, block)

    s_parts = row_parts(strip[1:])
    g_parts = row_parts(lower[1:])

    e0_rows = lax.dynamic_slice_in_dim(e0, r * run, run, 0)
    e1_rows = lax.dynamic_slice_in_dim(e1, r * run, run, 0)

    y0 = mm_t(e0, s0)
    r1 = s1.T - mm(f, y0)
    y1 = mm(e1_rows, r1)
    y = jnp.concatenate([lax.dynamic_slice_in_dim(y0, r * run, run, 0), y1], axis=0)
    share = 2 * run // n_col
    zt = lax.all_to_all(y.reshape(n_col, share, width), "col", split_axis=0, concat_axis=0, tiled=True)
    zt = zt.transpose(1, 0, 2).reshape(share, 2 * block)
    c0 = mm_t(zt[:, :block], e0)
    c1 = mm_t(zt[:, block:] - mm_t(c0, f), e1)
    ct = lax.all_gather(jnp.concatenate([c0, c1], axis=1), "col", axis=0, tiled=True)

    x_rows = mm(mm(e1_rows, f), e0)

    def columns(m, s):
        return lax.dynamic_slice_in_dim(m, lax.rem(r + s, n_row) * run, run, 1)

    z0 = 0.0
    z1 = 0.0
    for s, part in enumerate(s_parts):
        part = part.reshape(tail, 2, run)
        z0 = z0 + mm_t(part[:, 0, :], columns(e0_rows, s))
        z1 = z1 + mm_t(part[:, 1, :], columns(e1_rows, s)) - mm_t(part[:, 0, :], columns(x_rows, s))
    out = jnp.concatenate([z0, z1], axis=1)
    for s, part in enumerate(g_parts):
        part = part.reshape(tail, 2, run)
        out = out - mm_t(part[:, 0, :], columns(ct[:, :block], s))
        out = out - mm_t(part[:, 1, :], columns(ct[:, block:], s))
    lead = lax.dynamic_slice_in_dim(ct, c * width, width, 1).T
    reduced = jnp.concatenate([lead, out], axis=0)
    return reduced.reshape(rounds, width, 2, run)


def solution(mesh):
    spec = P(None, "col", None, "row")
    return jax.shard_map(local, mesh=mesh, in_specs=(spec, spec), out_specs=spec, check_vma=False)
```

```python
import jax
import jax.numpy as jnp
from jax import lax
from jax.sharding import PartitionSpec as P

PREC = lax.Precision.HIGH


def mm(a, b):
    return jnp.dot(a, b, precision=PREC, preferred_element_type=jnp.float32)


def mm_t(a, b):
    return lax.dot_general(
        a, b, (((1,), (1,)), ((), ())), precision=PREC, preferred_element_type=jnp.float32
    )


def row_parts(x):
    n = lax.axis_size("row")
    parts = [x]
    for s in range(1, n):
        parts.append(lax.ppermute(x, "row", [((i + s) % n, i) for i in range(n)]))
    return parts


def in_order(parts, r):
    n = len(parts)
    twice = jnp.stack(parts + parts[:-1], axis=0)
    return lax.dynamic_slice_in_dim(twice, (n - r) % n, n, 0)


def local(strip, lower):
    rounds, width, _, run = strip.shape
    n_row = lax.axis_size("row")
    n_col = lax.axis_size("col")
    block = run * n_row
    r = lax.axis_index("row")
    c = lax.axis_index("col")
    half = n_col // 2

    lead_l = lower[0]
    e1_mine = lead_l[:, 1, :]
    cut = width // 2
    moved = lax.ppermute(e1_mine[:cut], "col", [(half + i, i) for i in range(half)])
    e1_share = jnp.where(c < half, moved, e1_mine[cut:])
    packed = jnp.concatenate([lead_l[:, 0, :], e1_share], axis=0)
    whole = lax.all_gather(packed, ("row", "col"), axis=0)
    first_rounds = rounds // 2
    s_early = row_parts(strip[1:first_rounds])
    whole, s_early = lax.optimization_barrier((whole, s_early))
    whole = whole.reshape(n_row, n_col, width + cut, run)
    e0, f, e1 = [], [], []
    for k in range(n_row):
        first = whole[k, :, :width].reshape(2 * block, run)
        e0.append(first[:block])
        f.append(first[block:])
        second = whole[k, :, width:].reshape(2, half, cut, run)
        e1.append(second.transpose(1, 0, 2, 3).reshape(block, run))

    lead_s = in_order(row_parts(strip[0]), r)
    s0 = [lead_s[k, :, 0, :] for k in range(n_row)]
    s1 = [lead_s[k, :, 1, :] for k in range(n_row)]

    s_late = row_parts(strip[first_rounds:])
    g_parts = row_parts(lower[1:first_rounds]), row_parts(lower[first_rounds:])

    def cut_rows(m, k):
        return m[k * run:(k + 1) * run]

    def cut_cols(m, k):
        return m[:, k * run:(k + 1) * run]

    def total(terms):
        out = terms[0]
        for term in terms[1:]:
            out = out + term
        return out

    here = range(n_row)

    def own_rows(m):
        return lax.dynamic_slice_in_dim(m, r * run, run, 0)

    e0_rows = [own_rows(m) for m in e0]
    e1_rows = [own_rows(m) for m in e1]

    y0 = total([mm_t(e0[k], s0[k]) for k in here])
    r1 = jnp.concatenate([m.T for m in s1], axis=0) - total([mm(f[k], cut_rows(y0, k)) for k in here])
    y1 = total([mm(e1_rows[k], cut_rows(r1, k)) for k in here])
    y = jnp.concatenate([own_rows(y0), y1], axis=0)
    share = 2 * run // n_col
    zt = lax.all_to_all(y.reshape(n_col, share, width), "col", split_axis=0, concat_axis=0, tiled=True)
    zt, s_late = lax.optimization_barrier((zt, s_late))
    zt = zt.transpose(1, 0, 2).reshape(share, 2 * block)
    c0 = total([mm_t(cut_cols(zt, k), e0[k]) for k in here])
    rest = zt[:, block:] - total([mm_t(cut_cols(c0, k), f[k]) for k in here])
    c1 = total([mm_t(cut_cols(rest, k), e1[k]) for k in here])
    ct = lax.all_gather(jnp.concatenate([c0, c1], axis=1), "col", axis=0, tiled=True)
    ct, g_parts = lax.optimization_barrier((ct, g_parts))

    h = [total([mm(e1_rows[k], cut_rows(f[j], k)) for k in here]) for j in here]
    x_rows = [total([mm(h[k], cut_rows(e0[j], k)) for k in here]) for j in here]

    def along(parts, s):
        return lax.dynamic_index_in_dim(jnp.stack(parts), lax.rem(r + s, n_row), 0, keepdims=False)

    def columns(m, s):
        return lax.dynamic_slice_in_dim(m, lax.rem(r + s, n_row) * run, run, 1)

    lead = lax.dynamic_slice_in_dim(ct, c * width, width, 1).T
    pieces = [lead]
    for s_some, g_some in ((s_early, g_parts[0]), (s_late, g_parts[1])):
        z0 = 0.0
        z1 = 0.0
        for s, part in enumerate(s_some):
            part = part.reshape(-1, 2, run)
            z0 = z0 + mm_t(part[:, 0, :], along(e0_rows, s))
            z1 = z1 + mm_t(part[:, 1, :], along(e1_rows, s)) - mm_t(part[:, 0, :], along(x_rows, s))
        out = jnp.concatenate([z0, z1], axis=1)
        for s, part in enumerate(g_some):
            part = part.reshape(-1, 2, run)
            out = out - mm_t(part[:, 0, :], columns(ct[:, :block], s))
            out = out - mm_t(part[:, 1, :], columns(ct[:, block:], s))
        pieces.append(out)
    reduced = jnp.concatenate(pieces, axis=0)
    return reduced.reshape(rounds, width, 2, run)


def solution(mesh):
    spec = P(None, "col", None, "row")
    return jax.shard_map(local, mesh=mesh, in_specs=(spec, spec), out_specs=spec, check_vma=False)
```

```python
import functools

import jax
import jax.numpy as jnp
from jax import lax
from jax.experimental import pallas as pl
from jax.experimental.pallas import tpu as pltpu
from jax.sharding import PartitionSpec as P

PREC = lax.Precision.HIGH


def mm(a, b):
    return jnp.dot(a, b, precision=PREC, preferred_element_type=jnp.float32)


def mm_t(a, b):
    return lax.dot_general(
        a, b, (((1,), (1,)), ((), ())), precision=PREC, preferred_element_type=jnp.float32
    )


def row_parts(x):
    n = lax.axis_size("row")
    parts = [x]
    for s in range(1, n):
        parts.append(lax.ppermute(x, "row", [((i + s) % n, i) for i in range(n)]))
    return parts


def in_order(parts, r):
    n = len(parts)
    twice = jnp.stack(parts + parts[:-1], axis=0)
    return lax.dynamic_slice_in_dim(twice, (n - r) % n, n, 0)


def split(x):
    high = x.astype(jnp.bfloat16)
    return high, (x - high.astype(jnp.float32)).astype(jnp.bfloat16)


def below_kernel(n_row, chunks, *refs):
    ct_ref, lead_ref, mine_ref = refs[:3]
    z_refs = refs[3:3 + chunks]
    g_refs = refs[3 + chunks:3 + chunks * n_row]
    out_ref, high_ref, low_ref = refs[3 + chunks * n_row:]
    step = pl.program_id(0)
    per, width, _, run = out_ref.shape

    @pl.when(step == 0)
    def _():
        high, low = split(ct_ref[...])
        high_ref[...] = high
        low_ref[...] = low
        for b in range(2):
            out_ref[0, :, b, :] = lead_ref[:, b * run:(b + 1) * run]

    def chunk(q):
        skip = 1 if q == 0 else 0
        rows = (per - skip) * width
        sources = [(mine_ref, skip)] + [(g_refs[q * (n_row - 1) + s], 0) for s in range(n_row - 1)]
        pieces = []
        for ref, start in sources:
            for b in range(2):
                pieces.append(ref[start:, :, b, :].reshape(rows, run))
        high, low = split(jnp.concatenate(pieces, axis=1))

        def dot(a, b):
            return lax.dot_general(a, b, (((1,), (1,)), ((), ())), preferred_element_type=jnp.float32)

        for b in range(2):
            cols = slice(b * run, (b + 1) * run)
            c_high, c_low = high_ref[cols, :], low_ref[cols, :]
            update = dot(high, c_low) + dot(low, c_high) + dot(high, c_high)
            result = z_refs[q][:, cols] - update
            out_ref[skip:, :, b, :] = result.reshape(per - skip, width, run)

    for q in range(chunks):
        pl.when(step == q)(functools.partial(chunk, q))


def below(ct, lead, lower, z_parts, g_others):
    rounds, width, _, run = lower.shape
    chunks = len(z_parts)
    n_row = len(g_others[0]) + 1
    per = rounds // chunks

    def fixed(x):
        return pl.BlockSpec(x.shape, lambda i: (0,) * x.ndim, pipeline_mode=pl.Buffered(1))

    flat = [g for some in g_others for g in some]
    moving = pl.BlockSpec((per, width, 2, run), lambda i: (i, 0, 0, 0))
    return pl.pallas_call(
        functools.partial(below_kernel, n_row, chunks),
        grid=(chunks,),
        out_shape=jax.ShapeDtypeStruct(lower.shape, jnp.float32),
        in_specs=[fixed(ct), fixed(lead), moving] + [fixed(x) for x in z_parts] + [fixed(x) for x in flat],
        out_specs=moving,
        scratch_shapes=[pltpu.VMEM(ct.shape, jnp.bfloat16), pltpu.VMEM(ct.shape, jnp.bfloat16)],
        compiler_params=pltpu.CompilerParams(vmem_limit_bytes=56 * 1024 * 1024),
    )(ct, lead, lower, *z_parts, *flat)


def local(strip, lower):
    rounds, width, _, run = strip.shape
    n_row = lax.axis_size("row")
    n_col = lax.axis_size("col")
    block = run * n_row
    r = lax.axis_index("row")
    c = lax.axis_index("col")
    half = n_col // 2

    lead_l = lower[0]
    e1_mine = lead_l[:, 1, :]
    cut = width // 2
    moved = lax.ppermute(e1_mine[:cut], "col", [(half + i, i) for i in range(half)])
    e1_share = jnp.where(c < half, moved, e1_mine[cut:])
    packed = jnp.concatenate([lead_l[:, 0, :], e1_share], axis=0)
    whole = lax.all_gather(packed, ("row", "col"), axis=0)
    chunks = 3
    per = rounds // chunks
    s_parts = [row_parts(strip[q * per:(q + 1) * per]) for q in range(chunks)]
    g_others = [row_parts(lower[max(q * per, 1):(q + 1) * per])[1:] for q in range(chunks)]
    whole, s_parts[0], s_parts[1] = lax.optimization_barrier((whole, s_parts[0], s_parts[1]))
    whole = whole.reshape(n_row, n_col, width + cut, run)
    e0, f, e1 = [], [], []
    for k in range(n_row):
        first = whole[k, :, :width].reshape(2 * block, run)
        e0.append(first[:block])
        f.append(first[block:])
        second = whole[k, :, width:].reshape(2, half, cut, run)
        e1.append(second.transpose(1, 0, 2, 3).reshape(block, run))

    lead_s = in_order([part[0] for part in s_parts[0]], r)
    s0 = [lead_s[k, :, 0, :] for k in range(n_row)]
    s1 = [lead_s[k, :, 1, :] for k in range(n_row)]

    def cut_rows(m, k):
        return m[k * run:(k + 1) * run]

    def cut_cols(m, k):
        return m[:, k * run:(k + 1) * run]

    def total(terms):
        out = terms[0]
        for term in terms[1:]:
            out = out + term
        return out

    here = range(n_row)

    def own_rows(m):
        return lax.dynamic_slice_in_dim(m, r * run, run, 0)

    e0_rows = [own_rows(m) for m in e0]
    e1_rows = [own_rows(m) for m in e1]

    y0 = total([mm_t(e0[k], s0[k]) for k in here])
    r1 = jnp.concatenate([m.T for m in s1], axis=0) - total([mm(f[k], cut_rows(y0, k)) for k in here])
    y1 = total([mm(e1_rows[k], cut_rows(r1, k)) for k in here])
    y = jnp.concatenate([own_rows(y0), y1], axis=0)
    share = 2 * run // n_col
    zt = lax.all_to_all(y.reshape(n_col, share, width), "col", split_axis=0, concat_axis=0, tiled=True)
    zt, s_parts[2], g_others[0] = lax.optimization_barrier((zt, s_parts[2], g_others[0]))
    zt = zt.transpose(1, 0, 2).reshape(share, 2 * block)
    c0 = total([mm_t(cut_cols(zt, k), e0[k]) for k in here])
    rest = zt[:, block:] - total([mm_t(cut_cols(c0, k), f[k]) for k in here])
    c1 = total([mm_t(cut_cols(rest, k), e1[k]) for k in here])
    c0, c1, g_others[1] = lax.optimization_barrier((c0, c1, g_others[1]))
    c_pieces = []
    for s in here:
        start = lax.rem(r + s, n_row) * run
        c_pieces += [lax.dynamic_slice_in_dim(m, start, run, 1) for m in (c0, c1)]
    ct = lax.all_gather(jnp.concatenate(c_pieces, axis=1), "col", axis=0, tiled=True)
    ct, g_others[2] = lax.optimization_barrier((ct, g_others[2]))

    h = [total([mm(e1_rows[k], cut_rows(f[j], k)) for k in here]) for j in here]
    x_rows = [total([mm(h[k], cut_rows(e0[j], k)) for k in here]) for j in here]

    def along(parts, s):
        return lax.dynamic_index_in_dim(jnp.stack(parts), lax.rem(r + s, n_row), 0, keepdims=False)

    row_at = c * width
    part_at = lax.rem(lax.rem(row_at, block) // run - r + n_row, n_row)
    lead_at = part_at * 2 * run + (row_at // block) * run + lax.rem(row_at, run)
    lead = lax.dynamic_slice_in_dim(ct, lead_at, width, 1).T
    e0_near = [along(e0_rows, s) for s in here]
    e1_near = [along(e1_rows, s) for s in here]
    x_near = [along(x_rows, s) for s in here]
    z_parts = []
    for q in range(chunks):
        z0 = 0.0
        z1 = 0.0
        for s, part in enumerate(s_parts[q]):
            part = part[1:] if q == 0 else part
            part = part.reshape(-1, 2, run)
            z0 = z0 + mm_t(part[:, 0, :], e0_near[s])
            z1 = z1 + mm_t(part[:, 1, :], e1_near[s]) - mm_t(part[:, 0, :], x_near[s])
        z_parts.append(jnp.concatenate([z0, z1], axis=1))
    return below(ct, lead, lower, z_parts, g_others)


def solution(mesh):
    spec = P(None, "col", None, "row")
    return jax.shard_map(local, mesh=mesh, in_specs=(spec, spec), out_specs=spec, check_vma=False)
```

```python
import functools

import jax
import jax.numpy as jnp
from jax import lax
from jax.experimental import pallas as pl
from jax.experimental.pallas import tpu as pltpu
from jax.sharding import PartitionSpec as P

PREC = lax.Precision.HIGH


def mm(a, b):
    return jnp.dot(a, b, precision=PREC, preferred_element_type=jnp.float32)


def mm_t(a, b):
    return lax.dot_general(
        a, b, (((1,), (1,)), ((), ())), precision=PREC, preferred_element_type=jnp.float32
    )


def row_parts(x):
    n = lax.axis_size("row")
    parts = [x]
    for s in range(1, n):
        parts.append(lax.ppermute(x, "row", [((i + s) % n, i) for i in range(n)]))
    return parts


def in_order(parts, r):
    n = len(parts)
    twice = jnp.stack(parts + parts[:-1], axis=0)
    return lax.dynamic_slice_in_dim(twice, (n - r) % n, n, 0)


def split(x):
    high = x.astype(jnp.bfloat16)
    return high, (x - high.astype(jnp.float32)).astype(jnp.bfloat16)


def below_kernel(n_row, chunks, *refs):
    ct_ref, lead_ref, mine_ref = refs[:3]
    z_refs = refs[3:3 + chunks]
    g_refs = refs[3 + chunks:3 + chunks * n_row]
    out_ref, high_ref, low_ref = refs[3 + chunks * n_row:]
    step = pl.program_id(0)
    per, width, _, run = out_ref.shape

    @pl.when(step == 0)
    def _():
        high, low = split(ct_ref[...])
        high_ref[...] = high
        low_ref[...] = low
        for b in range(2):
            out_ref[0, :, b, :] = lead_ref[:, b * run:(b + 1) * run]

    def chunk(q):
        skip = 1 if q == 0 else 0
        rows = (per - skip) * width
        sources = [(mine_ref, skip)] + [(g_refs[q * (n_row - 1) + s], 0) for s in range(n_row - 1)]
        pieces = []
        for ref, start in sources:
            for b in range(2):
                pieces.append(ref[start:, :, b, :].reshape(rows, run))
        high, low = split(jnp.concatenate(pieces, axis=1))

        def dot(a, b):
            return lax.dot_general(a, b, (((1,), (1,)), ((), ())), preferred_element_type=jnp.float32)

        for b in range(2):
            cols = slice(b * run, (b + 1) * run)
            c_high, c_low = high_ref[cols, :], low_ref[cols, :]
            update = dot(high, c_low) + dot(low, c_high) + dot(high, c_high)
            result = z_refs[q][:, cols] - update
            out_ref[skip:, :, b, :] = result.reshape(per - skip, width, run)

    for q in range(chunks):
        pl.when(step == q)(functools.partial(chunk, q))


def below(ct, lead, lower, z_parts, g_others):
    rounds, width, _, run = lower.shape
    chunks = len(z_parts)
    n_row = len(g_others[0]) + 1
    per = rounds // chunks

    def fixed(x):
        return pl.BlockSpec(x.shape, lambda i: (0,) * x.ndim, pipeline_mode=pl.Buffered(1))

    flat = [g for some in g_others for g in some]
    moving = pl.BlockSpec((per, width, 2, run), lambda i: (i, 0, 0, 0))
    return pl.pallas_call(
        functools.partial(below_kernel, n_row, chunks),
        grid=(chunks,),
        out_shape=jax.ShapeDtypeStruct(lower.shape, jnp.float32),
        in_specs=[fixed(ct), fixed(lead), moving] + [fixed(x) for x in z_parts] + [fixed(x) for x in flat],
        out_specs=moving,
        scratch_shapes=[pltpu.VMEM(ct.shape, jnp.bfloat16), pltpu.VMEM(ct.shape, jnp.bfloat16)],
        compiler_params=pltpu.CompilerParams(vmem_limit_bytes=56 * 1024 * 1024),
    )(ct, lead, lower, *z_parts, *flat)


def local(strip, lower):
    rounds, width, _, run = strip.shape
    n_row = lax.axis_size("row")
    n_col = lax.axis_size("col")
    block = run * n_row
    r = lax.axis_index("row")
    c = lax.axis_index("col")
    half = n_col // 2

    lead_l = lower[0]
    e1_mine = lead_l[:, 1, :]
    cut = width // 2
    moved = lax.ppermute(e1_mine[:cut], "col", [(half + i, i) for i in range(half)])
    e1_share = jnp.where(c < half, moved, e1_mine[cut:])
    packed = jnp.concatenate([lead_l[:, 0, :], e1_share], axis=0)
    whole = lax.all_gather(packed, ("row", "col"), axis=0)
    chunks = 3
    per = rounds // chunks
    s_parts = [row_parts(strip[q * per:(q + 1) * per]) for q in range(chunks)]
    g_others = [row_parts(lower[max(q * per, 1):(q + 1) * per])[1:] for q in range(chunks)]
    whole, s_parts[0] = lax.optimization_barrier((whole, s_parts[0]))
    whole = whole.reshape(n_row, n_col, width + cut, run)
    e0, f, e1 = [], [], []
    for k in range(n_row):
        first = whole[k, :, :width].reshape(2 * block, run)
        e0.append(first[:block])
        f.append(first[block:])
        second = whole[k, :, width:].reshape(2, half, cut, run)
        e1.append(second.transpose(1, 0, 2, 3).reshape(block, run))

    lead_s = in_order([part[0] for part in s_parts[0]], r)
    s0 = [lead_s[k, :, 0, :] for k in range(n_row)]
    s1 = [lead_s[k, :, 1, :] for k in range(n_row)]

    def cut_rows(m, k):
        return m[k * run:(k + 1) * run]

    def cut_cols(m, k):
        return m[:, k * run:(k + 1) * run]

    def total(terms):
        out = terms[0]
        for term in terms[1:]:
            out = out + term
        return out

    here = range(n_row)

    def own_rows(m):
        return lax.dynamic_slice_in_dim(m, r * run, run, 0)

    e0_rows = [own_rows(m) for m in e0]
    e1_rows = [own_rows(m) for m in e1]

    y0 = total([mm_t(e0[k], s0[k]) for k in here])
    r1 = jnp.concatenate([m.T for m in s1], axis=0) - total([mm(f[k], cut_rows(y0, k)) for k in here])
    y1 = total([mm(e1_rows[k], cut_rows(r1, k)) for k in here])
    y = jnp.concatenate([own_rows(y0), y1], axis=0)
    share = 2 * run // n_col
    zt = lax.all_to_all(y.reshape(n_col, share, width), "col", split_axis=0, concat_axis=0, tiled=True)
    zt, s_parts[1], s_parts[2] = lax.optimization_barrier((zt, s_parts[1], s_parts[2]))
    zt = zt.transpose(1, 0, 2).reshape(share, 2 * block)
    c0 = total([mm_t(cut_cols(zt, k), e0[k]) for k in here])
    rest = zt[:, block:] - total([mm_t(cut_cols(c0, k), f[k]) for k in here])
    c1 = total([mm_t(cut_cols(rest, k), e1[k]) for k in here])
    c0, c1, g_others[0] = lax.optimization_barrier((c0, c1, g_others[0]))
    c_pieces = []
    for s in here:
        start = lax.rem(r + s, n_row) * run
        c_pieces += [lax.dynamic_slice_in_dim(m, start, run, 1) for m in (c0, c1)]
    ct = lax.all_gather(jnp.concatenate(c_pieces, axis=1), "col", axis=0, tiled=True)
    ct, g_others[1], g_others[2] = lax.optimization_barrier((ct, g_others[1], g_others[2]))

    h = [total([mm(e1_rows[k], cut_rows(f[j], k)) for k in here]) for j in here]
    x_rows = [total([mm(h[k], cut_rows(e0[j], k)) for k in here]) for j in here]

    def along(parts, s):
        return lax.dynamic_index_in_dim(jnp.stack(parts), lax.rem(r + s, n_row), 0, keepdims=False)

    row_at = c * width
    part_at = lax.rem(lax.rem(row_at, block) // run - r + n_row, n_row)
    lead_at = part_at * 2 * run + (row_at // block) * run + lax.rem(row_at, run)
    wanted = lax.broadcasted_iota(jnp.int32, (width, 2 * block), 0) + lead_at
    picks = (lax.broadcasted_iota(jnp.int32, (width, 2 * block), 1) == wanted).astype(jnp.float32)
    lead = lax.dot_general(
        picks, ct, (((1,), (1,)), ((), ())),
        precision=lax.Precision.HIGHEST, preferred_element_type=jnp.float32,
    )
    e0_near = [along(e0_rows, s) for s in here]
    e1_near = [along(e1_rows, s) for s in here]
    x_near = [along(x_rows, s) for s in here]
    z_parts = []
    for q in range(chunks):
        z0 = 0.0
        z1 = 0.0
        for s, part in enumerate(s_parts[q]):
            part = part[1:] if q == 0 else part
            part = part.reshape(-1, 2, run)
            z0 = z0 + mm_t(part[:, 0, :], e0_near[s])
            z1 = z1 + mm_t(part[:, 1, :], e1_near[s]) - mm_t(part[:, 0, :], x_near[s])
        z_parts.append(jnp.concatenate([z0, z1], axis=1))
    return below(ct, lead, lower, z_parts, g_others)


def solution(mesh):
    spec = P(None, "col", None, "row")
    return jax.shard_map(local, mesh=mesh, in_specs=(spec, spec), out_specs=spec, check_vma=False)
```

```python
import functools

import jax
import jax.numpy as jnp
from jax import lax
from jax.experimental import pallas as pl
from jax.experimental.pallas import tpu as pltpu
from jax.sharding import PartitionSpec as P

PREC = lax.Precision.HIGH


def mm(a, b):
    return jnp.dot(a, b, precision=PREC, preferred_element_type=jnp.float32)


def mm_t(a, b):
    return lax.dot_general(
        a, b, (((1,), (1,)), ((), ())), precision=PREC, preferred_element_type=jnp.float32
    )


def row_parts(x):
    n = lax.axis_size("row")
    parts = [x]
    for s in range(1, n):
        parts.append(lax.ppermute(x, "row", [((i + s) % n, i) for i in range(n)]))
    return parts


def in_order(parts, r):
    n = len(parts)
    twice = jnp.stack(parts + parts[:-1], axis=0)
    return lax.dynamic_slice_in_dim(twice, (n - r) % n, n, 0)


def split(x):
    high = x.astype(jnp.bfloat16)
    return high, (x - high.astype(jnp.float32)).astype(jnp.bfloat16)


def below_kernel(n_row, chunks, *refs):
    ct_ref, lead_ref, mine_ref = refs[:3]
    z_refs = refs[3:3 + chunks]
    g_refs = refs[3 + chunks:3 + chunks * n_row]
    out_ref, high_ref, low_ref = refs[3 + chunks * n_row:]
    step = pl.program_id(0)
    per, width, _, run = out_ref.shape

    @pl.when(step == 0)
    def _():
        high, low = split(ct_ref[...])
        high_ref[...] = high
        low_ref[...] = low
        for b in range(2):
            out_ref[0, :, b, :] = lead_ref[:, b * run:(b + 1) * run]

    def chunk(q):
        skip = 1 if q == 0 else 0
        rows = (per - skip) * width
        sources = [(mine_ref, skip)] + [(g_refs[q * (n_row - 1) + s], 0) for s in range(n_row - 1)]
        pieces = []
        for ref, start in sources:
            for b in range(2):
                pieces.append(ref[start:, :, b, :].reshape(rows, run))
        high, low = split(jnp.concatenate(pieces, axis=1))

        def dot(a, b):
            return lax.dot_general(a, b, (((1,), (1,)), ((), ())), preferred_element_type=jnp.float32)

        for b in range(2):
            cols = slice(b * run, (b + 1) * run)
            c_high, c_low = high_ref[cols, :], low_ref[cols, :]
            update = dot(high, c_low) + dot(low, c_high) + dot(high, c_high)
            result = z_refs[q][:, cols] - update
            out_ref[skip:, :, b, :] = result.reshape(per - skip, width, run)

    for q in range(chunks):
        pl.when(step == q)(functools.partial(chunk, q))


def below(ct, lead, lower, z_parts, g_others):
    rounds, width, _, run = lower.shape
    chunks = len(z_parts)
    n_row = len(g_others[0]) + 1
    per = rounds // chunks

    def fixed(x):
        return pl.BlockSpec(x.shape, lambda i: (0,) * x.ndim, pipeline_mode=pl.Buffered(1))

    flat = [g for some in g_others for g in some]
    moving = pl.BlockSpec((per, width, 2, run), lambda i: (i, 0, 0, 0))
    return pl.pallas_call(
        functools.partial(below_kernel, n_row, chunks),
        grid=(chunks,),
        out_shape=jax.ShapeDtypeStruct(lower.shape, jnp.float32),
        in_specs=[fixed(ct), fixed(lead), moving] + [fixed(x) for x in z_parts] + [fixed(x) for x in flat],
        out_specs=moving,
        scratch_shapes=[pltpu.VMEM(ct.shape, jnp.bfloat16), pltpu.VMEM(ct.shape, jnp.bfloat16)],
        compiler_params=pltpu.CompilerParams(vmem_limit_bytes=56 * 1024 * 1024),
    )(ct, lead, lower, *z_parts, *flat)


def local(strip, lower):
    rounds, width, _, run = strip.shape
    n_row = lax.axis_size("row")
    n_col = lax.axis_size("col")
    block = run * n_row
    r = lax.axis_index("row")
    c = lax.axis_index("col")
    half = n_col // 2

    lead_l = lower[0]
    e1_mine = lead_l[:, 1, :]
    cut = width // 2
    moved = lax.ppermute(e1_mine[:cut], "col", [(half + i, i) for i in range(half)])
    e1_share = jnp.where(c < half, moved, e1_mine[cut:])
    packed = jnp.concatenate([lead_l[:, 0, :], e1_share], axis=0)
    whole = lax.all_gather(packed, ("row", "col"), axis=0)
    chunks = 3
    per = rounds // chunks
    s_parts = [row_parts(strip[q * per:(q + 1) * per]) for q in range(chunks)]
    g_others = [row_parts(lower[max(q * per, 1):(q + 1) * per])[1:] for q in range(chunks)]
    whole, s_parts[0] = lax.optimization_barrier((whole, s_parts[0]))
    whole = whole.reshape(n_row, n_col, width + cut, run)
    e0, f, e1 = [], [], []
    for k in range(n_row):
        first = whole[k, :, :width].reshape(2 * block, run)
        e0.append(first[:block])
        f.append(first[block:])
        second = whole[k, :, width:].reshape(2, half, cut, run)
        e1.append(second.transpose(1, 0, 2, 3).reshape(block, run))

    lead_s = in_order([part[0] for part in s_parts[0]], r)
    s0 = [lead_s[k, :, 0, :] for k in range(n_row)]
    s1 = [lead_s[k, :, 1, :] for k in range(n_row)]

    def cut_rows(m, k):
        return m[k * run:(k + 1) * run]

    def cut_cols(m, k):
        return m[:, k * run:(k + 1) * run]

    def total(terms):
        out = terms[0]
        for term in terms[1:]:
            out = out + term
        return out

    here = range(n_row)

    def own_rows(m):
        return lax.dynamic_slice_in_dim(m, r * run, run, 0)

    e0_rows = [own_rows(m) for m in e0]
    e1_rows = [own_rows(m) for m in e1]

    y0 = total([mm_t(e0[k], s0[k]) for k in here])
    r1 = jnp.concatenate([m.T for m in s1], axis=0) - total([mm(f[k], cut_rows(y0, k)) for k in here])
    y1 = total([mm(e1_rows[k], cut_rows(r1, k)) for k in here])
    y = jnp.concatenate([own_rows(y0), y1], axis=0)
    share = 2 * run // n_col
    zt = lax.all_to_all(y.reshape(n_col, share, width), "col", split_axis=0, concat_axis=0, tiled=True)
    zt, s_parts[1], s_parts[2] = lax.optimization_barrier((zt, s_parts[1], s_parts[2]))
    zt = zt.transpose(1, 0, 2).reshape(share, 2 * block)
    c0 = total([mm_t(cut_cols(zt, k), e0[k]) for k in here])
    rest = zt[:, block:] - total([mm_t(cut_cols(c0, k), f[k]) for k in here])
    c1 = total([mm_t(cut_cols(rest, k), e1[k]) for k in here])
    c0, c1, g_others[0] = lax.optimization_barrier((c0, c1, g_others[0]))
    c_pieces = []
    for s in here:
        start = lax.rem(r + s, n_row) * run
        c_pieces += [lax.dynamic_slice_in_dim(m, start, run, 1) for m in (c0, c1)]
    ct = lax.all_gather(jnp.concatenate(c_pieces, axis=1), "col", axis=0, tiled=True)
    ct, g_others[1] = lax.optimization_barrier((ct, g_others[1]))

    h = [total([mm(e1_rows[k], cut_rows(f[j], k)) for k in here]) for j in here]
    x_rows = [total([mm(h[k], cut_rows(e0[j], k)) for k in here]) for j in here]

    def along(parts, s):
        return lax.dynamic_index_in_dim(jnp.stack(parts), lax.rem(r + s, n_row), 0, keepdims=False)

    row_at = c * width
    part_at = lax.rem(lax.rem(row_at, block) // run - r + n_row, n_row)
    lead_at = part_at * 2 * run + (row_at // block) * run + lax.rem(row_at, run)
    wanted = lax.broadcasted_iota(jnp.int32, (width, 2 * block), 0) + lead_at
    picks = (lax.broadcasted_iota(jnp.int32, (width, 2 * block), 1) == wanted).astype(jnp.float32)
    lead = lax.dot_general(
        picks, ct, (((1,), (1,)), ((), ())),
        precision=lax.Precision.HIGHEST, preferred_element_type=jnp.float32,
    )
    lead, g_others[2] = lax.optimization_barrier((lead, g_others[2]))
    e0_near = [along(e0_rows, s) for s in here]
    e1_near = [along(e1_rows, s) for s in here]
    x_near = [along(x_rows, s) for s in here]
    z_parts = []
    for q in range(chunks):
        z0 = 0.0
        z1 = 0.0
        for s, part in enumerate(s_parts[q]):
            part = part[1:] if q == 0 else part
            part = part.reshape(-1, 2, run)
            z0 = z0 + mm_t(part[:, 0, :], e0_near[s])
            z1 = z1 + mm_t(part[:, 1, :], e1_near[s]) - mm_t(part[:, 0, :], x_near[s])
        z_parts.append(jnp.concatenate([z0, z1], axis=1))
    return below(ct, lead, lower, z_parts, g_others)


def solution(mesh):
    spec = P(None, "col", None, "row")
    return jax.shard_map(local, mesh=mesh, in_specs=(spec, spec), out_specs=spec, check_vma=False)
```
